32 devices in a mesh: band: 2 (over y), domain: 16 (over z, x, core).
Axes of the slice: x: 2, y: 2, z: 4, core: 2. Of those that a mesh axis runs over, the one named last changes fastest.
Arguments:
- targets: float32 [4, 36864, 192], P('band', 'domain'), may hold values from -5 to 5
- partner_pool: bfloat16 [64, 36864, 192], P('band', 'domain'), may hold values from -5 to 5
- owners: int32 [2], replicated, may hold values from 0 to 1, as said below
- warm_start: bfloat16 [2, 8, 4, 36864, 192], P(None, None, 'band', 'domain'), may hold values from -6 to 6
Outputs:
- exchange: float32 [4, 36864, 192], P('band', 'domain')
The draws below stay inside these ranges and needn't reach their ends.
Inputs may be any that keep to these rules, and one draw needn't show every extreme that they name: The 2 broadcast blocks have distinct owners.
All inputs are finite; a program needn't handle non-finite values.
Results may differ from the reference program's by a relative error of at most 0.0006.
Values may be sent and summed in bfloat16 or wider, within the bound.
A program may use at most 576 MiB of HBM per device.

```python
import math
import jax
import jax.numpy as jnp
from jax import lax

ORB = 8
POOL = 4
STEPS = 2
SWEEPS = 3
TGT = 2
GX = 192
GY = 192
GZ = 192
GROUPS = 2


def orbital_field(key, row_count):
    key_jitter, key_offset = jax.random.split(key, 2)
    position = (jnp.arange(GX * GY, dtype=jnp.int32) // GY).astype(jnp.float32) / GX
    jitter = jnp.clip(jax.random.normal(key_jitter, (row_count, GX * GY, GZ), jnp.float32), -5.0, 5.0)
    offset = jax.random.uniform(key_offset, (row_count, 1, 1), jnp.float32, -0.8, 0.8)
    envelope = 0.5 + position
    return 0.5 * envelope[None, :, None] * (offset + jitter)


def draw_targets(key, part):
    return orbital_field(jax.random.fold_in(key, 11), GROUPS * TGT)


def draw_partner_pool(key, part):
    return orbital_field(jax.random.fold_in(key, 23), GROUPS * POOL * ORB).astype(jnp.bfloat16)


def draw_owners(key, part):
    shuffled = jax.random.permutation(jax.random.fold_in(key, 37), jnp.arange(GROUPS, dtype=jnp.int32))
    return shuffled[:STEPS]


def steps_of(own_key, shape, shards, smallest, high):
    level = 1.0
    for dim, blocks in shards:
        heights = jax.random.uniform(jax.random.fold_in(jax.random.fold_in(own_key, 6), dim), (blocks,), jnp.float32, smallest / len(shards), high / len(shards))
        level = level * jnp.repeat(jnp.exp(heights), shape[dim] // blocks).reshape((-1,) + (1,) * (len(shape) - 1 - dim))
    return level


def gaussian(own_key, extent, width, limit, shards=(), kind=jnp.bfloat16):
    factor_of = steps_of(own_key, extent, shards, -0.22, 0.18) if shards else 1.0
    values = jax.random.normal(own_key, extent, jnp.float32) * width * factor_of
    return jnp.minimum(jnp.maximum(values, -limit), limit).astype(kind)


def setup_inputs(seed: int = 0) -> dict:
    key_of = jax.random.split(jax.random.key(seed), 5)
    targets = draw_targets(jax.random.fold_in(key_of[4], 71), 0)
    partner_pool = draw_partner_pool(jax.random.fold_in(key_of[4], 71), 0)
    owners = draw_owners(jax.random.fold_in(key_of[4], 71), 0)
    warm_start = gaussian(key_of[3], (STEPS, ORB, GROUPS * TGT, GX * GY, GZ), 1.0, 6.0, ((2, 2), (3, 16)))
    return dict(targets=targets, partner_pool=partner_pool, owners=owners, warm_start=warm_start)


coupling = 4.0 * math.pi


def jacobi(potential, source):
    beside = jnp.roll(potential, 1, 1) + jnp.roll(potential, -1, 1)
    beside = beside + jnp.roll(potential, 1, 2) + jnp.roll(potential, -1, 2)
    beside = beside + jnp.roll(potential, 1, 3) + jnp.roll(potential, -1, 3)
    return (beside + coupling * source) / 6.0


def reference(targets, partner_pool, owners, warm_start):
    grid_shape = (GX, GY, GZ)
    cell_count = GX * GY * GZ
    exchange = jnp.zeros(targets.shape, jnp.float32)
    for block_index in range(STEPS):
        first_row = (owners[block_index] * POOL + block_index) * ORB
        partner = lax.dynamic_slice_in_dim(partner_pool, first_row.astype(jnp.int32), ORB, 0)
        partner = partner.astype(jnp.float32).reshape((ORB,) + grid_shape)
        warm_block = warm_start[block_index]

        def one_target(target_index):
            target = lax.dynamic_index_in_dim(targets, target_index, 0, keepdims=False).reshape(grid_shape)
            start_field = lax.dynamic_index_in_dim(warm_block, target_index, 1, keepdims=False)
            start_field = start_field.reshape((ORB,) + grid_shape)
            density = partner * target[None]
            mean_value = jnp.sum(density, axis=(1, 2, 3), keepdims=True) / cell_count
            source = density - mean_value
            potential = start_field.astype(jnp.float32)
            for sweep_index in range(SWEEPS):
                potential = jacobi(potential, source)
            return jnp.sum(potential * partner, axis=0).reshape(targets.shape[1:])

        contribution = lax.map(one_target, jnp.arange(GROUPS * TGT, dtype=jnp.int32))
        exchange = exchange - contribution
    return exchange
```

```python
import functools
import math

import jax
import jax.numpy as jnp
from jax import lax
from jax.experimental import pallas as pl
from jax.experimental.pallas import tpu as pltpu
from jax.sharding import PartitionSpec as P

ORB = 8
STEPS = 2
SWEEPS = 3
GX = 192
GY = 192
GZ = 192


coupling = 4.0 * math.pi


def spread(block, axis, owner):
    block = jnp.where(lax.axis_index(axis) == owner, block, jnp.zeros_like(block))
    return lax.psum(block, axis)


def padded(block, sides, width):
    for axis, dim in sides:
        count = lax.axis_size(axis)
        forward = [(i, i + 1) for i in range(count - 1)]
        forward.append((count - 1, 0))
        backward = [(target, source) for source, target in forward]
        low = lax.ppermute(
            lax.slice_in_dim(block, block.shape[dim] - width, None, axis=dim), axis, forward
        )
        high = lax.ppermute(lax.slice_in_dim(block, 0, width, axis=dim), axis, backward)
        block = jnp.concatenate([low, block, high], axis=dim)
    return block


def row_sweep(widened, source, first_row):
    row_count = source.shape[1]
    line = GY
    centre = widened[:, line : line + row_count]
    beside = widened[:, :row_count] + widened[:, 2 * line : 2 * line + row_count]
    column = (first_row + jnp.arange(row_count, dtype=jnp.int32)) % line
    at_end = (column == line - 1)[None, :, None]
    at_start = (column == 0)[None, :, None]
    upper = jnp.where(
        at_end, widened[:, 1 : row_count + 1], widened[:, line + 1 : line + row_count + 1]
    )
    lower = jnp.where(
        at_start,
        widened[:, 2 * line - 1 : 2 * line - 1 + row_count],
        widened[:, line - 1 : line - 1 + row_count],
    )
    beside = beside + upper + lower + jnp.roll(centre, 1, 2) + jnp.roll(centre, -1, 2)
    return (beside + coupling * source) / 6.0


def fetch_block(partner_pool, owners, block_index):
    own_block = partner_pool[block_index * ORB : (block_index + 1) * ORB]
    return spread(own_block, "band", owners[block_index]).astype(jnp.float32)


def pair_products(partner, targets):
    density = partner[:, None] * targets[None]
    return (density, jnp.sum(density, axis=(2, 3)))


def solve_block(partner, density, mean_value, warm_block, first_row):
    block_width = partner.shape[0]
    target_count = density.shape[1]
    pair_count = block_width * target_count
    planes = density.shape[2:]
    source = density.reshape((pair_count,) + planes) - mean_value.reshape(pair_count, 1, 1)
    potential = warm_block.reshape((pair_count,) + planes).astype(jnp.float32)
    for sweep_index in range(SWEEPS):
        widened = padded(potential.astype(jnp.bfloat16), (("domain", 1),), GY).astype(
            potential.dtype
        )
        potential = row_sweep(widened, source, first_row)
    potential = potential.reshape((block_width, target_count) + planes)
    return jnp.sum(potential * partner[:, None], axis=0)


def sweep_body(targets, partner_pool, owners, warm_start):
    row_count = targets.shape[1]
    first_row = lax.axis_index("domain") * row_count
    cell_count = GX * GY * GZ
    exchange = jnp.zeros(targets.shape, jnp.float32)
    for block_index in range(STEPS):
        partner = fetch_block(partner_pool, owners, block_index)
        density, local_sums = pair_products(partner, targets)
        totals = lax.psum(local_sums, "domain")
        exchange = exchange - solve_block(
            partner, density, totals / cell_count, warm_start[block_index], first_row
        )
    return exchange


EDGE = SWEEPS


def coupled(centre, ring):
    return jnp.dot(ring, centre, preferred_element_type=jnp.float32) + jnp.dot(
        centre, ring, preferred_element_type=jnp.float32
    )


def sums_kernel(planes, low_ref, mid_ref, high_ref, targets_ref, sums_ref):
    mid = planes - 2 * EDGE

    def add(piece, index, plane, totals):
        partner = piece[0, index].astype(jnp.float32)
        return tuple(
            total + jnp.sum((partner * targets_ref[j, plane]).reshape(-1, 8, GZ), axis=0)
            for j, total in enumerate(totals)
        )

    totals = tuple(jnp.zeros((8, GZ), jnp.float32) for _ in range(targets_ref.shape[0]))
    totals = lax.fori_loop(0, EDGE, lambda k, t: add(low_ref, k, k, t), totals)
    totals = lax.fori_loop(0, mid, lambda k, t: add(mid_ref, k, k + EDGE, t), totals)
    totals = lax.fori_loop(0, EDGE, lambda k, t: add(high_ref, k, k + EDGE + mid, t), totals)
    for j, total in enumerate(totals):
        sums_ref[0, j] = total


def pair_sums(pieces, targets):
    count, planes = targets.shape[:2]
    out = pl.pallas_call(
        functools.partial(sums_kernel, planes),
        grid=(ORB,),
        in_specs=[
            pl.BlockSpec((1,) + piece.shape[1:], lambda i: (i, 0, 0, 0)) for piece in pieces
        ]
        + [pl.BlockSpec(targets.shape, lambda i: (0, 0, 0, 0), pipeline_mode=pl.Buffered(1))],
        out_specs=pl.BlockSpec((1, count, 8, GZ), lambda i: (i, 0, 0, 0)),
        out_shape=jax.ShapeDtypeStruct((ORB, count, 8, GZ), jnp.float32),
        cost_estimate=pl.CostEstimate(
            flops=2 * ORB * targets.size, bytes_accessed=11_000_000, transcendentals=0
        ),
        compiler_params=pltpu.CompilerParams(vmem_limit_bytes=40 << 20),
    )(*pieces, targets)
    return jnp.sum(out, axis=(2, 3))


def window_kernel(
    planes,
    step_ref,
    below_ref,
    low_ref,
    mid_ref,
    high_ref,
    above_ref,
    targets_ref,
    warm_ref,
    ring_ref,
    out_ref,
    partner,
    target,
    start,
    first,
    second,
):
    i, j = pl.program_id(0), pl.program_id(1)
    mid = planes - 2 * EDGE
    wide = planes + 2 * EDGE
    blank = jnp.zeros((GY, GZ), jnp.float32)

    @pl.when((i == 0) & (j == 0))
    def _():
        for t in range(targets_ref.shape[0]):
            for e in range(EDGE):
                target[t, e] = blank
                target[t, planes + EDGE + e] = blank

            def place(k, carry, t=t):
                target[t, k + EDGE] = targets_ref[t, k]
                return carry

            lax.fori_loop(0, planes, place, 0)

        def clear(k, carry):
            for t in range(targets_ref.shape[0]):
                out_ref[t, k] = blank
            return carry

        lax.fori_loop(0, wide, clear, 0)
        for e in range(EDGE + 1):
            start[e] = blank.astype(start.dtype)
            start[planes + EDGE + 1 + e] = blank.astype(start.dtype)
            first[e] = blank
            first[planes + EDGE + 1 + e] = blank
            second[e] = blank
            second[planes + EDGE + 1 + e] = blank

    @pl.when(j == 0)
    def _():
        place_at = 0
        for piece in (below_ref, low_ref, mid_ref, high_ref, above_ref):

            def place(k, carry, piece=piece, place_at=place_at):
                partner[place_at + k] = piece[0, k].astype(jnp.float32)
                return carry

            lax.fori_loop(0, piece.shape[1], place, 0)
            place_at += piece.shape[1]

    def load(k, carry):
        start[k + EDGE + 1] = warm_ref[0, 0, 0, k]
        return carry

    lax.fori_loop(0, planes, load, 0)
    ring = ring_ref[...]

    def swept(field, e, weight):
        centre = field[e + 1]
        beside = field[e].astype(jnp.float32) + field[e + 2].astype(jnp.float32)
        source = (partner[e] * weight) * target[j, e]
        return beside + source + coupled(centre.astype(jnp.bfloat16), ring)

    def sweep_one(n, carry):
        for half in range(2):
            e = 2 + 2 * n + half
            first[e + 1] = swept(start, e, coupling)
        return carry

    def sweep_two(n, carry):
        for half in range(2):
            e = 1 + 2 * n + half
            second[e + 1] = swept(first, e, 6.0 * coupling)
        return carry

    def sweep_three(n, carry):
        for half in range(2):
            e = 2 * n + half
            out_ref[j, e] += swept(second, e, 36.0 * coupling) * (partner[e] * (-1.0 / 216.0))
        return carry

    lax.fori_loop(0, (planes + 2) // 2, sweep_one, 0)
    lax.fori_loop(0, (planes + 4) // 2, sweep_two, 0)
    lax.fori_loop(0, (planes + 6) // 2, sweep_three, 0)


def window(step, below, pieces, above, targets, warm_start, ring):
    count, planes = targets.shape[:2]
    wide = planes + 2 * EDGE
    parts = (below,) + tuple(pieces) + (above,)
    plane = (GY, GZ)
    grid_spec = pltpu.PrefetchScalarGridSpec(
        num_scalar_prefetch=1,
        grid=(ORB, count),
        in_specs=[
            pl.BlockSpec((1,) + part.shape[1:], lambda i, j, s: (i, 0, 0, 0)) for part in parts
        ]
        + [
            pl.BlockSpec(targets.shape, lambda i, j, s: (0, 0, 0, 0), pipeline_mode=pl.Buffered(1)),
            pl.BlockSpec((1, 1, 1, planes) + plane, lambda i, j, s: (s[0], i, j, 0, 0, 0)),
            pl.BlockSpec(plane, lambda i, j, s: (0, 0), pipeline_mode=pl.Buffered(1)),
        ],
        out_specs=pl.BlockSpec((count, wide) + plane, lambda i, j, s: (0, 0, 0, 0), pipeline_mode=pl.Buffered(1)),
        scratch_shapes=[
            pltpu.VMEM((wide,) + plane, jnp.float32),
            pltpu.VMEM((count, wide) + plane, jnp.float32),
            pltpu.VMEM((wide + 2,) + plane, jnp.bfloat16),
            pltpu.VMEM((wide + 2,) + plane, jnp.float32),
            pltpu.VMEM((wide + 2,) + plane, jnp.float32),
        ],
    )
    return pl.pallas_call(
        functools.partial(window_kernel, planes),
        grid_spec=grid_spec,
        out_shape=jax.ShapeDtypeStruct((count, wide) + plane, jnp.float32),
        cost_estimate=pl.CostEstimate(
            flops=ORB * count * 48 * 4 * GY * GY * GZ, bytes_accessed=30_000_000, transcendentals=0
        ),
        compiler_params=pltpu.CompilerParams(vmem_limit_bytes=56 << 20),
    )(step.reshape(1), *parts, targets, warm_start, ring)


def final_kernel(planes, means_ref, *refs):
    own, remote, own_low, own_high, remote_low, remote_high = refs[:6]
    pieces = (refs[6:9], refs[9:12])
    out_ref = refs[12]
    k = pl.program_id(0)
    count = out_ref.shape[0]
    for j in range(count):
        out_ref[j, 0] = own[j, 0] + remote[j, 0]

    def constants(which):
        for j in range(count):
            total = out_ref[j, 0]
            for block in range(2):
                for i in range(ORB):
                    total += means_ref[block * ORB + i, j] * pieces[block][which][i, 0].astype(
                        jnp.float32
                    )
            out_ref[j, 0] = total

    @pl.when(k < EDGE)
    def _():
        for j in range(count):
            out_ref[j, 0] += own_low[j, 0] + remote_low[j, 0]
        constants(0)

    @pl.when((k >= EDGE) & (k < planes - EDGE))
    def _():
        constants(1)

    @pl.when(k >= planes - EDGE)
    def _():
        for j in range(count):
            out_ref[j, 0] += own_high[j, 0] + remote_high[j, 0]
        constants(2)


def final_sum(means, own, remote, sides, own_pieces, remote_pieces):
    count, wide = own.shape[:2]
    planes = wide - 2 * EDGE
    plane = (GY, GZ)
    mid = planes - 2 * EDGE
    at_low = lambda k: (0, jnp.minimum(k, EDGE - 1), 0, 0)
    at_mid = lambda k: (0, jnp.clip(k - EDGE, 0, mid - 1), 0, 0)
    at_high = lambda k: (0, jnp.maximum(k - (planes - EDGE), 0), 0, 0)
    centre = pl.BlockSpec((count, 1) + plane, lambda k: (0, k + EDGE, 0, 0))
    side = [pl.BlockSpec((count, 1) + plane, at) for at in (at_low, at_high)]
    piece = [pl.BlockSpec((ORB, 1) + plane, at) for at in (at_low, at_mid, at_high)]
    return pl.pallas_call(
        functools.partial(final_kernel, planes),
        grid=(planes,),
        in_specs=[pl.BlockSpec(memory_space=pltpu.SMEM), centre, centre] + side + side + piece + piece,
        out_specs=pl.BlockSpec((count, 1) + plane, lambda k: (0, k, 0, 0)),
        out_shape=jax.ShapeDtypeStruct((count, planes) + plane, jnp.float32),
        cost_estimate=pl.CostEstimate(
            flops=40 * count * planes * GY * GZ, bytes_accessed=28_000_000, transcendentals=0
        ),
        compiler_params=pltpu.CompilerParams(vmem_limit_bytes=40 << 20),
    )(means, own, remote, *sides, *own_pieces, *remote_pieces)


def plane_body(targets, partner_pool, owners, warm_start):
    count, rows = targets.shape[:2]
    planes = rows // GY
    plane = (GY, GZ)
    targets = targets.reshape((count, planes) + plane)
    pool = partner_pool.reshape((partner_pool.shape[0], planes) + plane)
    warm = warm_start.reshape((STEPS, ORB, count, planes) + plane)
    devices = lax.axis_size("domain")
    upward = [(d, (d + 1) % devices) for d in range(devices)]
    downward = [(d, (d - 1) % devices) for d in range(devices)]
    swap = [(0, 1), (1, 0)]
    band = lax.axis_index("band")
    own_step = jnp.where(owners[0] == band, 0, 1).astype(jnp.int32)
    mid = planes - 2 * EDGE

    def cut(at, size):
        return lax.dynamic_slice(pool, (own_step * ORB, at, 0, 0), (ORB, size) + plane)

    own_pieces = (cut(0, EDGE), cut(EDGE, mid), cut(planes - EDGE, EDGE))
    low, middle, high = own_pieces
    far_low = lax.ppermute(low, "band", swap)
    far_high = lax.ppermute(high, "band", swap)
    far_mid = lax.ppermute(middle, "band", swap)
    far_pieces = (far_low, far_mid, far_high)
    below = lax.ppermute(high, "domain", upward)
    above = lax.ppermute(low, "domain", downward)
    far_below = lax.ppermute(far_high, "domain", upward)
    far_above = lax.ppermute(far_low, "domain", downward)

    index = jnp.arange(GY, dtype=jnp.int32)
    apart = (index[:, None] - index[None, :]) % GY
    ring = ((apart == 1) | (apart == GY - 1)).astype(jnp.bfloat16)

    def sent(field):
        to_above = lax.ppermute(field[:, planes + EDGE :], "domain", upward)
        to_below = lax.ppermute(field[:, :EDGE], "domain", downward)
        return (to_above, to_below)

    own_sums = pair_sums(own_pieces, targets)
    own = window(own_step, below, own_pieces, above, targets, warm, ring)
    own_sides = sent(own)
    far_sums = pair_sums(far_pieces, targets)
    totals = lax.psum(jnp.concatenate([own_sums, far_sums], axis=0), "domain")
    means = totals * (coupling / (2.0 * GX * GY * GZ))
    far = window(1 - own_step, far_below, far_pieces, far_above, targets, warm, ring)
    far_sides = sent(far)
    out = final_sum(means, own, far, own_sides + far_sides, own_pieces, far_pieces)
    return out.reshape(count, rows, GZ)


def body(targets, partner_pool, owners, warm_start):
    rows = targets.shape[1]
    planes = rows // GY
    whole_planes = rows % GY == 0 and planes % 2 == 0 and planes > 2 * EDGE
    if whole_planes and GY == GZ and lax.axis_size("band") == 2:
        return plane_body(targets, partner_pool, owners, warm_start)
    return sweep_body(targets, partner_pool, owners, warm_start)


def solution(mesh):
    return jax.shard_map(
        body,
        mesh=mesh,
        in_specs=(
            P("band", "domain", None),
            P("band", "domain", None),
            P(),
            P(None, None, "band", "domain", None),
        ),
        out_specs=P("band", "domain", None),
        check_vma=False,
    )
```

```python
import functools
import math

import jax
import jax.numpy as jnp
from jax import lax
from jax.experimental import pallas as pl
from jax.experimental.pallas import tpu as pltpu
from jax.sharding import PartitionSpec as P

ORB = 8
STEPS = 2
SWEEPS = 3
GX = 192
GY = 192
GZ = 192


coupling = 4.0 * math.pi


def spread(block, axis, owner):
    block = jnp.where(lax.axis_index(axis) == owner, block, jnp.zeros_like(block))
    return lax.psum(block, axis)


def padded(block, sides, width):
    for axis, dim in sides:
        count = lax.axis_size(axis)
        forward = [(i, i + 1) for i in range(count - 1)]
        forward.append((count - 1, 0))
        backward = [(target, source) for source, target in forward]
        low = lax.ppermute(
            lax.slice_in_dim(block, block.shape[dim] - width, None, axis=dim), axis, forward
        )
        high = lax.ppermute(lax.slice_in_dim(block, 0, width, axis=dim), axis, backward)
        block = jnp.concatenate([low, block, high], axis=dim)
    return block


def row_sweep(widened, source, first_row):
    row_count = source.shape[1]
    line = GY
    centre = widened[:, line : line + row_count]
    beside = widened[:, :row_count] + widened[:, 2 * line : 2 * line + row_count]
    column = (first_row + jnp.arange(row_count, dtype=jnp.int32)) % line
    at_end = (column == line - 1)[None, :, None]
    at_start = (column == 0)[None, :, None]
    upper = jnp.where(
        at_end, widened[:, 1 : row_count + 1], widened[:, line + 1 : line + row_count + 1]
    )
    lower = jnp.where(
        at_start,
        widened[:, 2 * line - 1 : 2 * line - 1 + row_count],
        widened[:, line - 1 : line - 1 + row_count],
    )
    beside = beside + upper + lower + jnp.roll(centre, 1, 2) + jnp.roll(centre, -1, 2)
    return (beside + coupling * source) / 6.0


def fetch_block(partner_pool, owners, block_index):
    own_block = partner_pool[block_index * ORB : (block_index + 1) * ORB]
    return spread(own_block, "band", owners[block_index]).astype(jnp.float32)


def pair_products(partner, targets):
    density = partner[:, None] * targets[None]
    return (density, jnp.sum(density, axis=(2, 3)))


def solve_block(partner, density, mean_value, warm_block, first_row):
    block_width = partner.shape[0]
    target_count = density.shape[1]
    pair_count = block_width * target_count
    planes = density.shape[2:]
    source = density.reshape((pair_count,) + planes) - mean_value.reshape(pair_count, 1, 1)
    potential = warm_block.reshape((pair_count,) + planes).astype(jnp.float32)
    for sweep_index in range(SWEEPS):
        widened = padded(potential.astype(jnp.bfloat16), (("domain", 1),), GY).astype(
            potential.dtype
        )
        potential = row_sweep(widened, source, first_row)
    potential = potential.reshape((block_width, target_count) + planes)
    return jnp.sum(potential * partner[:, None], axis=0)


def sweep_body(targets, partner_pool, owners, warm_start):
    row_count = targets.shape[1]
    first_row = lax.axis_index("domain") * row_count
    cell_count = GX * GY * GZ
    exchange = jnp.zeros(targets.shape, jnp.float32)
    for block_index in range(STEPS):
        partner = fetch_block(partner_pool, owners, block_index)
        density, local_sums = pair_products(partner, targets)
        totals = lax.psum(local_sums, "domain")
        exchange = exchange - solve_block(
            partner, density, totals / cell_count, warm_start[block_index], first_row
        )
    return exchange


EDGE = SWEEPS


def coupled(centre, ring):
    return jnp.dot(ring, centre, preferred_element_type=jnp.float32) + jnp.dot(
        centre, ring, preferred_element_type=jnp.float32
    )


def sums_kernel(planes, low_ref, mid_ref, high_ref, targets_ref, sums_ref):
    mid = planes - 2 * EDGE

    def add(piece, index, plane, totals):
        partner = piece[0, index].astype(jnp.float32)
        return tuple(
            total + jnp.sum((partner * targets_ref[j, plane]).reshape(-1, 8, GZ), axis=0)
            for j, total in enumerate(totals)
        )

    totals = tuple(jnp.zeros((8, GZ), jnp.float32) for _ in range(targets_ref.shape[0]))
    totals = lax.fori_loop(0, EDGE, lambda k, t: add(low_ref, k, k, t), totals)
    totals = lax.fori_loop(0, mid, lambda k, t: add(mid_ref, k, k + EDGE, t), totals)
    totals = lax.fori_loop(0, EDGE, lambda k, t: add(high_ref, k, k + EDGE + mid, t), totals)
    for j, total in enumerate(totals):
        sums_ref[0, j] = total


def pair_sums(pieces, targets):
    count, planes = targets.shape[:2]
    out = pl.pallas_call(
        functools.partial(sums_kernel, planes),
        grid=(ORB,),
        in_specs=[
            pl.BlockSpec((1,) + piece.shape[1:], lambda i: (i, 0, 0, 0)) for piece in pieces
        ]
        + [pl.BlockSpec(targets.shape, lambda i: (0, 0, 0, 0), pipeline_mode=pl.Buffered(1))],
        out_specs=pl.BlockSpec((1, count, 8, GZ), lambda i: (i, 0, 0, 0)),
        out_shape=jax.ShapeDtypeStruct((ORB, count, 8, GZ), jnp.float32),
        cost_estimate=pl.CostEstimate(
            flops=2 * ORB * targets.size, bytes_accessed=11_000_000, transcendentals=0
        ),
        compiler_params=pltpu.CompilerParams(vmem_limit_bytes=40 << 20),
    )(*pieces, targets)
    return jnp.sum(out, axis=(2, 3))


def window_kernel(
    planes,
    step_ref,
    below_ref,
    low_ref,
    mid_ref,
    high_ref,
    above_ref,
    targets_ref,
    warm_ref,
    ring_ref,
    out_ref,
    partner,
    target,
    start,
    first,
    second,
):
    i, j = pl.program_id(0), pl.program_id(1)
    mid = planes - 2 * EDGE
    wide = planes + 2 * EDGE
    blank = jnp.zeros((GY, GZ), jnp.float32)

    @pl.when((i == 0) & (j == 0))
    def _():
        for t in range(targets_ref.shape[0]):
            for e in range(EDGE):
                target[t, e] = blank
                target[t, planes + EDGE + e] = blank

            def place(k, carry, t=t):
                target[t, k + EDGE] = targets_ref[t, k]
                return carry

            lax.fori_loop(0, planes, place, 0)

        def clear(k, carry):
            for t in range(targets_ref.shape[0]):
                out_ref[t, k] = blank
            return carry

        lax.fori_loop(0, wide, clear, 0)
        for e in range(EDGE + 1):
            start[e] = blank.astype(start.dtype)
            start[planes + EDGE + 1 + e] = blank.astype(start.dtype)
            first[e] = blank
            first[planes + EDGE + 1 + e] = blank
            second[e] = blank
            second[planes + EDGE + 1 + e] = blank

    @pl.when(j == 0)
    def _():
        place_at = 0
        for piece in (below_ref, low_ref, mid_ref, high_ref, above_ref):

            def place(k, carry, piece=piece, place_at=place_at):
                partner[place_at + k] = piece[0, k].astype(jnp.float32)
                return carry

            lax.fori_loop(0, piece.shape[1], place, 0)
            place_at += piece.shape[1]

    for k in range(planes):
        start[k + EDGE + 1] = warm_ref[0, 0, 0, :, k * GY : (k + 1) * GY]
    ring = ring_ref[...]

    def swept(field, e, weight):
        centre = field[e + 1]
        beside = field[e].astype(jnp.float32) + field[e + 2].astype(jnp.float32)
        source = (partner[e] * weight) * target[j, e]
        return beside + source + coupled(centre.astype(jnp.bfloat16), ring)

    def sweep_one(n, carry):
        for half in range(2):
            e = 2 + 2 * n + half
            first[e + 1] = swept(start, e, coupling)
        return carry

    def sweep_two(n, carry):
        for half in range(2):
            e = 1 + 2 * n + half
            second[e + 1] = swept(first, e, 6.0 * coupling)
        return carry

    def sweep_three(n, carry):
        for half in range(2):
            e = 2 * n + half
            out_ref[j, e] += swept(second, e, 36.0 * coupling) * (partner[e] * (-1.0 / 216.0))
        return carry

    lax.fori_loop(0, (planes + 2) // 2, sweep_one, 0)
    lax.fori_loop(0, (planes + 4) // 2, sweep_two, 0)
    lax.fori_loop(0, (planes + 6) // 2, sweep_three, 0)


def window(step, orbitals, below, pieces, above, targets, warm_start, ring):
    first, number = orbitals
    count, planes = targets.shape[:2]
    wide = planes + 2 * EDGE
    parts = (below,) + tuple(pieces) + (above,)
    plane = (GY, GZ)
    grid_spec = pltpu.PrefetchScalarGridSpec(
        num_scalar_prefetch=1,
        grid=(number, count),
        in_specs=[
            pl.BlockSpec((1,) + part.shape[1:], lambda i, j, s: (first + i, 0, 0, 0)) for part in parts
        ]
        + [
            pl.BlockSpec(targets.shape, lambda i, j, s: (0, 0, 0, 0), pipeline_mode=pl.Buffered(1)),
            pl.BlockSpec((1, 1, 1, GZ, planes * GY), lambda i, j, s: (s[0], first + i, j, 0, 0)),
            pl.BlockSpec(plane, lambda i, j, s: (0, 0), pipeline_mode=pl.Buffered(1)),
        ],
        out_specs=pl.BlockSpec((count, wide) + plane, lambda i, j, s: (0, 0, 0, 0), pipeline_mode=pl.Buffered(1)),
        scratch_shapes=[
            pltpu.VMEM((wide,) + plane, jnp.float32),
            pltpu.VMEM((count, wide) + plane, jnp.float32),
            pltpu.VMEM((wide + 2,) + plane, jnp.bfloat16),
            pltpu.VMEM((wide + 2,) + plane, jnp.float32),
            pltpu.VMEM((wide + 2,) + plane, jnp.float32),
        ],
    )
    return pl.pallas_call(
        functools.partial(window_kernel, planes),
        grid_spec=grid_spec,
        out_shape=jax.ShapeDtypeStruct((count, wide) + plane, jnp.float32),
        cost_estimate=pl.CostEstimate(
            flops=number * count * 80 * 4 * GY * GY * GZ, bytes_accessed=4_000_000 * number, transcendentals=0
        ),
        compiler_params=pltpu.CompilerParams(vmem_limit_bytes=56 << 20),
    )(step.reshape(1), *parts, targets, warm_start, ring)


def final_kernel(planes, means_ref, *refs):
    own, more, remote, own_low, own_high, remote_low, remote_high = refs[:7]
    pieces = (refs[7:10], refs[10:13])
    out_ref = refs[13]
    k = pl.program_id(0)
    count = out_ref.shape[0]
    for j in range(count):
        out_ref[j, 0] = own[j, 0] + more[j, 0] + remote[j, 0]

    def constants(which):
        for j in range(count):
            total = out_ref[j, 0]
            for block in range(2):
                for i in range(ORB):
                    total += means_ref[block * ORB + i, j] * pieces[block][which][i, 0].astype(
                        jnp.float32
                    )
            out_ref[j, 0] = total

    @pl.when(k < EDGE)
    def _():
        for j in range(count):
            out_ref[j, 0] += own_low[j, 0] + remote_low[j, 0]
        constants(0)

    @pl.when((k >= EDGE) & (k < planes - EDGE))
    def _():
        constants(1)

    @pl.when(k >= planes - EDGE)
    def _():
        for j in range(count):
            out_ref[j, 0] += own_high[j, 0] + remote_high[j, 0]
        constants(2)


def final_sum(means, own, more, remote, sides, own_pieces, remote_pieces):
    count, wide = own.shape[:2]
    planes = wide - 2 * EDGE
    plane = (GY, GZ)
    mid = planes - 2 * EDGE
    at_low = lambda k: (0, jnp.minimum(k, EDGE - 1), 0, 0)
    at_mid = lambda k: (0, jnp.clip(k - EDGE, 0, mid - 1), 0, 0)
    at_high = lambda k: (0, jnp.maximum(k - (planes - EDGE), 0), 0, 0)
    centre = pl.BlockSpec((count, 1) + plane, lambda k: (0, k + EDGE, 0, 0))
    side = [pl.BlockSpec((count, 1) + plane, at) for at in (at_low, at_high)]
    piece = [pl.BlockSpec((ORB, 1) + plane, at) for at in (at_low, at_mid, at_high)]
    return pl.pallas_call(
        functools.partial(final_kernel, planes),
        grid=(planes,),
        in_specs=[pl.BlockSpec(memory_space=pltpu.SMEM), centre, centre, centre] + side + side + piece + piece,
        out_specs=pl.BlockSpec((count, 1) + plane, lambda k: (0, k, 0, 0)),
        out_shape=jax.ShapeDtypeStruct((count, planes) + plane, jnp.float32),
        cost_estimate=pl.CostEstimate(
            flops=40 * count * planes * GY * GZ, bytes_accessed=28_000_000, transcendentals=0
        ),
        compiler_params=pltpu.CompilerParams(vmem_limit_bytes=40 << 20),
    )(means, own, more, remote, *sides, *own_pieces, *remote_pieces)


def by_plane(field, planes):
    return field.reshape(field.shape[0], GZ, planes, GY).transpose(0, 2, 1, 3)


def shifted_sum(values, shifts, devices):
    parts = [
        lax.ppermute(values, "domain", [(d, (d + shift) % devices) for d in range(devices)])
        for shift in shifts
    ]
    return functools.reduce(jnp.add, parts, values)


def plane_body(targets, partner_pool, owners, warm_start):
    count, rows = targets.shape[:2]
    planes = rows // GY
    plane = (GY, GZ)
    targets = by_plane(jnp.swapaxes(targets, 1, 2), planes)
    pool = jnp.swapaxes(partner_pool, 1, 2)
    warm = jnp.swapaxes(warm_start, 3, 4)
    devices = lax.axis_size("domain")
    upward = [(d, (d + 1) % devices) for d in range(devices)]
    downward = [(d, (d - 1) % devices) for d in range(devices)]
    swap = [(0, 1), (1, 0)]
    band = lax.axis_index("band")
    own_step = jnp.where(owners[0] == band, 0, 1).astype(jnp.int32)
    mid = planes - 2 * EDGE

    block = lax.dynamic_slice(pool, (own_step * ORB, 0, 0), (ORB, GZ, rows))
    block = by_plane(lax.optimization_barrier(block), planes)
    own_pieces = (block[:, :EDGE], block[:, EDGE : EDGE + mid], block[:, planes - EDGE :])
    low, middle, high = own_pieces
    far_low = lax.ppermute(low, "band", swap)
    far_high = lax.ppermute(high, "band", swap)
    far_mid = lax.ppermute(middle, "band", swap)
    below = lax.ppermute(high, "domain", upward)
    above = lax.ppermute(low, "domain", downward)

    index = jnp.arange(GY, dtype=jnp.int32)
    apart = (index[:, None] - index[None, :]) % GY
    ring = ((apart == 1) | (apart == GY - 1)).astype(jnp.bfloat16)

    def sent(field):
        to_above = lax.ppermute(field[:, EDGE:], "domain", upward)
        to_below = lax.ppermute(field[:, :EDGE], "domain", downward)
        return (to_above, to_below)

    half = ORB // 2
    own_sums = pair_sums(own_pieces, targets)
    below, own_sums = lax.optimization_barrier((below, own_sums))
    own = window(own_step, (0, half), below, own_pieces, above, targets, warm, ring)
    far_low, far_high, own = lax.optimization_barrier((far_low, far_high, own))
    far_below = lax.ppermute(far_high, "domain", upward)
    far_above = lax.ppermute(far_low, "domain", downward)
    below, own = lax.optimization_barrier((below, own))
    more = window(own_step, (half, half), below, own_pieces, above, targets, warm, ring)
    own_sides = sent(jnp.concatenate([own[:, :EDGE] + more[:, :EDGE], own[:, EDGE + planes :] + more[:, EDGE + planes :]], axis=1))
    far_mid, more = lax.optimization_barrier((far_mid, more))
    far_pieces = (far_low, far_mid, far_high)
    far_sums = pair_sums(far_pieces, targets)
    totals = jnp.concatenate([own_sums, far_sums], axis=0)
    totals = shifted_sum(totals, range(1, 4), devices)
    totals, far_below = lax.optimization_barrier((totals, far_below))
    totals = shifted_sum(totals, range(4, devices, 4), devices)
    means = totals * (coupling / (2.0 * GX * GY * GZ))
    far = window(1 - own_step, (0, ORB), far_below, far_pieces, far_above, targets, warm, ring)
    far_sides = sent(jnp.concatenate([far[:, :EDGE], far[:, EDGE + planes :]], axis=1))
    out = final_sum(means, own, more, far, own_sides + far_sides, own_pieces, far_pieces)
    out = out.transpose(0, 2, 1, 3).reshape(count, GZ, rows)
    return jnp.swapaxes(out, 1, 2)


def body(targets, partner_pool, owners, warm_start):
    rows = targets.shape[1]
    planes = rows // GY
    whole_planes = rows % GY == 0 and planes % 2 == 0 and planes > 2 * EDGE
    if whole_planes and GY == GZ and lax.axis_size("domain") % 4 == 0 and lax.axis_size("band") == 2:
        return plane_body(targets, partner_pool, owners, warm_start)
    return sweep_body(targets, partner_pool, owners, warm_start)


def solution(mesh):
    return jax.shard_map(
        body,
        mesh=mesh,
        in_specs=(
            P("band", "domain", None),
            P("band", "domain", None),
            P(),
            P(None, None, "band", "domain", None),
        ),
        out_specs=P("band", "domain", None),
        check_vma=False,
    )
```

```python
import functools
import math

import jax
import jax.numpy as jnp
from jax import lax
from jax.experimental import pallas as pl
from jax.experimental.pallas import tpu as pltpu
from jax.sharding import PartitionSpec as P

ORB = 8
STEPS = 2
SWEEPS = 3
GX = 192
GY = 192
GZ = 192


coupling = 4.0 * math.pi


def spread(block, axis, owner):
    block = jnp.where(lax.axis_index(axis) == owner, block, jnp.zeros_like(block))
    return lax.psum(block, axis)


def padded(block, sides, width):
    for axis, dim in sides:
        count = lax.axis_size(axis)
        forward = [(i, i + 1) for i in range(count - 1)]
        forward.append((count - 1, 0))
        backward = [(target, source) for source, target in forward]
        low = lax.ppermute(
            lax.slice_in_dim(block, block.shape[dim] - width, None, axis=dim), axis, forward
        )
        high = lax.ppermute(lax.slice_in_dim(block, 0, width, axis=dim), axis, backward)
        block = jnp.concatenate([low, block, high], axis=dim)
    return block


def row_sweep(widened, source, first_row):
    row_count = source.shape[1]
    line = GY
    centre = widened[:, line : line + row_count]
    beside = widened[:, :row_count] + widened[:, 2 * line : 2 * line + row_count]
    column = (first_row + jnp.arange(row_count, dtype=jnp.int32)) % line
    at_end = (column == line - 1)[None, :, None]
    at_start = (column == 0)[None, :, None]
    upper = jnp.where(
        at_end, widened[:, 1 : row_count + 1], widened[:, line + 1 : line + row_count + 1]
    )
    lower = jnp.where(
        at_start,
        widened[:, 2 * line - 1 : 2 * line - 1 + row_count],
        widened[:, line - 1 : line - 1 + row_count],
    )
    beside = beside + upper + lower + jnp.roll(centre, 1, 2) + jnp.roll(centre, -1, 2)
    return (beside + coupling * source) / 6.0


def fetch_block(partner_pool, owners, block_index):
    own_block = partner_pool[block_index * ORB : (block_index + 1) * ORB]
    return spread(own_block, "band", owners[block_index]).astype(jnp.float32)


def pair_products(partner, targets):
    density = partner[:, None] * targets[None]
    return (density, jnp.sum(density, axis=(2, 3)))


def solve_block(partner, density, mean_value, warm_block, first_row):
    block_width = partner.shape[0]
    target_count = density.shape[1]
    pair_count = block_width * target_count
    planes = density.shape[2:]
    source = density.reshape((pair_count,) + planes) - mean_value.reshape(pair_count, 1, 1)
    potential = warm_block.reshape((pair_count,) + planes).astype(jnp.float32)
    for sweep_index in range(SWEEPS):
        widened = padded(potential.astype(jnp.bfloat16), (("domain", 1),), GY).astype(
            potential.dtype
        )
        potential = row_sweep(widened, source, first_row)
    potential = potential.reshape((block_width, target_count) + planes)
    return jnp.sum(potential * partner[:, None], axis=0)


def sweep_body(targets, partner_pool, owners, warm_start):
    row_count = targets.shape[1]
    first_row = lax.axis_index("domain") * row_count
    cell_count = GX * GY * GZ
    exchange = jnp.zeros(targets.shape, jnp.float32)
    for block_index in range(STEPS):
        partner = fetch_block(partner_pool, owners, block_index)
        density, local_sums = pair_products(partner, targets)
        totals = lax.psum(local_sums, "domain")
        exchange = exchange - solve_block(
            partner, density, totals / cell_count, warm_start[block_index], first_row
        )
    return exchange


EDGE = SWEEPS


def coupled(centre, ring):
    return jnp.dot(ring, centre, preferred_element_type=jnp.float32) + jnp.dot(
        centre, ring, preferred_element_type=jnp.float32
    )


def sums_kernel(planes, low_ref, mid_ref, high_ref, targets_ref, sums_ref):
    mid = planes - 2 * EDGE

    def add(piece, index, plane, totals):
        partner = piece[0, index].astype(jnp.float32)
        return tuple(
            total + jnp.sum((partner * targets_ref[j, plane]).reshape(-1, 8, GZ), axis=0)
            for j, total in enumerate(totals)
        )

    totals = tuple(jnp.zeros((8, GZ), jnp.float32) for _ in range(targets_ref.shape[0]))
    totals = lax.fori_loop(0, EDGE, lambda k, t: add(low_ref, k, k, t), totals)
    totals = lax.fori_loop(0, mid, lambda k, t: add(mid_ref, k, k + EDGE, t), totals)
    totals = lax.fori_loop(0, EDGE, lambda k, t: add(high_ref, k, k + EDGE + mid, t), totals)
    for j, total in enumerate(totals):
        sums_ref[0, j] = total


def pair_sums(pieces, targets):
    count, planes = targets.shape[:2]
    out = pl.pallas_call(
        functools.partial(sums_kernel, planes),
        grid=(ORB,),
        in_specs=[
            pl.BlockSpec((1,) + piece.shape[1:], lambda i: (i, 0, 0, 0)) for piece in pieces
        ]
        + [pl.BlockSpec(targets.shape, lambda i: (0, 0, 0, 0), pipeline_mode=pl.Buffered(1))],
        out_specs=pl.BlockSpec((1, count, 8, GZ), lambda i: (i, 0, 0, 0)),
        out_shape=jax.ShapeDtypeStruct((ORB, count, 8, GZ), jnp.float32),
        cost_estimate=pl.CostEstimate(
            flops=2 * ORB * targets.size, bytes_accessed=11_000_000, transcendentals=0
        ),
        compiler_params=pltpu.CompilerParams(vmem_limit_bytes=40 << 20),
    )(*pieces, targets)
    return jnp.sum(out, axis=(2, 3))


def window_kernel(
    planes,
    step_ref,
    below_ref,
    low_ref,
    mid_ref,
    high_ref,
    above_ref,
    targets_ref,
    warm_ref,
    ring_ref,
    out_ref,
    partner,
    target,
    start,
    first,
    second,
):
    i, j = pl.program_id(0), pl.program_id(1)
    mid = planes - 2 * EDGE
    wide = planes + 2 * EDGE
    blank = jnp.zeros((GY, GZ), jnp.float32)

    @pl.when((i == 0) & (j == 0))
    def _():
        for t in range(targets_ref.shape[0]):
            for e in range(EDGE):
                target[t, e] = blank
                target[t, planes + EDGE + e] = blank

            def place(k, carry, t=t):
                target[t, k + EDGE] = targets_ref[t, k]
                return carry

            lax.fori_loop(0, planes, place, 0)

        def clear(k, carry):
            for t in range(targets_ref.shape[0]):
                out_ref[t, k] = blank
            return carry

        lax.fori_loop(0, wide, clear, 0)
        for e in range(EDGE + 1):
            start[e] = blank.astype(start.dtype)
            start[planes + EDGE + 1 + e] = blank.astype(start.dtype)
            first[e] = blank
            first[planes + EDGE + 1 + e] = blank
            second[e] = blank
            second[planes + EDGE + 1 + e] = blank

    @pl.when(j == 0)
    def _():
        place_at = 0
        for piece in (below_ref, low_ref, mid_ref, high_ref, above_ref):

            def place(k, carry, piece=piece, place_at=place_at):
                partner[place_at + k] = piece[0, k].astype(jnp.float32)
                return carry

            lax.fori_loop(0, piece.shape[1], place, 0)
            place_at += piece.shape[1]

    for k in range(planes):
        start[k + EDGE + 1] = warm_ref[0, 0, 0, :, k * GY : (k + 1) * GY]
    ring = ring_ref[...]

    def swept(field, e, weight):
        centre = field[e + 1]
        beside = field[e].astype(jnp.float32) + field[e + 2].astype(jnp.float32)
        source = (partner[e] * weight) * target[j, e]
        return beside + source + coupled(centre.astype(jnp.bfloat16), ring)

    def sweep_one(n, carry):
        for half in range(2):
            e = 2 + 2 * n + half
            first[e + 1] = swept(start, e, coupling)
        return carry

    def sweep_two(n, carry):
        for half in range(2):
            e = 1 + 2 * n + half
            second[e + 1] = swept(first, e, 6.0 * coupling)
        return carry

    def sweep_three(n, carry):
        for half in range(2):
            e = 2 * n + half
            out_ref[j, e] += swept(second, e, 36.0 * coupling) * (partner[e] * (-1.0 / 216.0))
        return carry

    lax.fori_loop(0, (planes + 2) // 2, sweep_one, 0)
    lax.fori_loop(0, (planes + 4) // 2, sweep_two, 0)
    lax.fori_loop(0, (planes + 6) // 2, sweep_three, 0)


def window(step, orbitals, below, pieces, above, targets, warm_start, ring):
    first, number = orbitals
    count, planes = targets.shape[:2]
    wide = planes + 2 * EDGE
    parts = (below,) + tuple(pieces) + (above,)
    plane = (GY, GZ)
    grid_spec = pltpu.PrefetchScalarGridSpec(
        num_scalar_prefetch=1,
        grid=(number, count),
        in_specs=[
            pl.BlockSpec((1,) + part.shape[1:], lambda i, j, s: (first + i, 0, 0, 0)) for part in parts
        ]
        + [
            pl.BlockSpec(targets.shape, lambda i, j, s: (0, 0, 0, 0), pipeline_mode=pl.Buffered(1)),
            pl.BlockSpec((1, 1, 1, GZ, planes * GY), lambda i, j, s: (s[0], first + i, j, 0, 0)),
            pl.BlockSpec(plane, lambda i, j, s: (0, 0), pipeline_mode=pl.Buffered(1)),
        ],
        out_specs=pl.BlockSpec((count, wide) + plane, lambda i, j, s: (0, 0, 0, 0), pipeline_mode=pl.Buffered(1)),
        scratch_shapes=[
            pltpu.VMEM((wide,) + plane, jnp.float32),
            pltpu.VMEM((count, wide) + plane, jnp.float32),
            pltpu.VMEM((wide + 2,) + plane, jnp.bfloat16),
            pltpu.VMEM((wide + 2,) + plane, jnp.float32),
            pltpu.VMEM((wide + 2,) + plane, jnp.float32),
        ],
    )
    return pl.pallas_call(
        functools.partial(window_kernel, planes),
        grid_spec=grid_spec,
        out_shape=jax.ShapeDtypeStruct((count, wide) + plane, jnp.float32),
        cost_estimate=pl.CostEstimate(
            flops=number * count * 80 * 4 * GY * GY * GZ, bytes_accessed=4_000_000 * number, transcendentals=0
        ),
        compiler_params=pltpu.CompilerParams(vmem_limit_bytes=56 << 20),
    )(step.reshape(1), *parts, targets, warm_start, ring)


def final_kernel(planes, means_ref, *refs):
    own, more, remote, own_low, own_high, remote_low, remote_high = refs[:7]
    pieces = (refs[7:10], refs[10:13])
    out_ref = refs[13]
    k = pl.program_id(0)
    count = out_ref.shape[0]
    for j in range(count):
        out_ref[j, 0] = own[j, 0] + more[j, 0] + remote[j, 0]

    def constants(which):
        for j in range(count):
            total = out_ref[j, 0]
            for block in range(2):
                for i in range(ORB):
                    total += means_ref[block * ORB + i, j] * pieces[block][which][i, 0].astype(
                        jnp.float32
                    )
            out_ref[j, 0] = total

    @pl.when(k < EDGE)
    def _():
        for j in range(count):
            out_ref[j, 0] += own_low[j, 0] + remote_low[j, 0]
        constants(0)

    @pl.when((k >= EDGE) & (k < planes - EDGE))
    def _():
        constants(1)

    @pl.when(k >= planes - EDGE)
    def _():
        for j in range(count):
            out_ref[j, 0] += own_high[j, 0] + remote_high[j, 0]
        constants(2)


def final_sum(means, own, more, remote, sides, own_pieces, remote_pieces):
    count, wide = own.shape[:2]
    planes = wide - 2 * EDGE
    plane = (GY, GZ)
    mid = planes - 2 * EDGE
    at_low = lambda k: (0, jnp.minimum(k, EDGE - 1), 0, 0)
    at_mid = lambda k: (0, jnp.clip(k - EDGE, 0, mid - 1), 0, 0)
    at_high = lambda k: (0, jnp.maximum(k - (planes - EDGE), 0), 0, 0)
    centre = pl.BlockSpec((count, 1) + plane, lambda k: (0, k + EDGE, 0, 0))
    side = [pl.BlockSpec((count, 1) + plane, at) for at in (at_low, at_high)]
    piece = [pl.BlockSpec((ORB, 1) + plane, at) for at in (at_low, at_mid, at_high)]
    return pl.pallas_call(
        functools.partial(final_kernel, planes),
        grid=(planes,),
        in_specs=[pl.BlockSpec(memory_space=pltpu.SMEM), centre, centre, centre] + side + side + piece + piece,
        out_specs=pl.BlockSpec((count, 1) + plane, lambda k: (0, k, 0, 0)),
        out_shape=jax.ShapeDtypeStruct((count, planes) + plane, jnp.float32),
        cost_estimate=pl.CostEstimate(
            flops=40 * count * planes * GY * GZ, bytes_accessed=28_000_000, transcendentals=0
        ),
        compiler_params=pltpu.CompilerParams(vmem_limit_bytes=40 << 20),
    )(means, own, more, remote, *sides, *own_pieces, *remote_pieces)


def by_plane(field, planes):
    return field.reshape(field.shape[0], GZ, planes, GY).transpose(0, 2, 1, 3)


def shifted_sum(values, shifts, devices):
    parts = [
        lax.ppermute(values, "domain", [(d, (d + shift) % devices) for d in range(devices)])
        for shift in shifts
    ]
    return functools.reduce(jnp.add, parts, values)


def plane_body(targets, partner_pool, owners, warm_start):
    count, rows = targets.shape[:2]
    planes = rows // GY
    plane = (GY, GZ)
    targets = by_plane(jnp.swapaxes(targets, 1, 2), planes)
    pool = jnp.swapaxes(partner_pool, 1, 2)
    warm = jnp.swapaxes(warm_start, 3, 4)
    devices = lax.axis_size("domain")
    upward = [(d, (d + 1) % devices) for d in range(devices)]
    downward = [(d, (d - 1) % devices) for d in range(devices)]
    swap = [(0, 1), (1, 0)]
    band = lax.axis_index("band")
    own_step = jnp.where(owners[0] == band, 0, 1).astype(jnp.int32)
    mid = planes - 2 * EDGE

    block = lax.dynamic_slice(pool, (own_step * ORB, 0, 0), (ORB, GZ, rows))
    block = lax.optimization_barrier(block)
    sides = EDGE * GY
    swapped = [
        by_plane(lax.ppermute(part, "band", swap), part.shape[2] // GY)
        for part in (block[:, :, :sides], block[:, :, rows - sides :], block[:, :, sides : rows - sides])
    ]
    far_low, far_high, far_mid = swapped
    block = by_plane(block, planes)
    own_pieces = (block[:, :EDGE], block[:, EDGE : EDGE + mid], block[:, planes - EDGE :])
    low, _, high = own_pieces
    below = lax.ppermute(high, "domain", upward)
    above = lax.ppermute(low, "domain", downward)

    index = jnp.arange(GY, dtype=jnp.int32)
    apart = (index[:, None] - index[None, :]) % GY
    ring = ((apart == 1) | (apart == GY - 1)).astype(jnp.bfloat16)

    def sent(field):
        to_above = lax.ppermute(field[:, EDGE:], "domain", upward)
        to_below = lax.ppermute(field[:, :EDGE], "domain", downward)
        return (to_above, to_below)

    half = ORB // 2
    own_sums = pair_sums(own_pieces, targets)
    below, own_sums = lax.optimization_barrier((below, own_sums))
    own = window(own_step, (0, half), below, own_pieces, above, targets, warm, ring)
    far_low, far_high, own = lax.optimization_barrier((far_low, far_high, own))
    far_below = lax.ppermute(far_high, "domain", upward)
    far_above = lax.ppermute(far_low, "domain", downward)
    below, own = lax.optimization_barrier((below, own))
    more = window(own_step, (half, half), below, own_pieces, above, targets, warm, ring)
    own_sides = sent(jnp.concatenate([own[:, :EDGE] + more[:, :EDGE], own[:, EDGE + planes :] + more[:, EDGE + planes :]], axis=1))
    far_mid, more = lax.optimization_barrier((far_mid, more))
    far_pieces = (far_low, far_mid, far_high)
    far_sums = pair_sums(far_pieces, targets)
    totals = jnp.concatenate([own_sums, far_sums], axis=0)
    totals = shifted_sum(totals, range(1, 4), devices)
    totals = shifted_sum(totals, range(4, devices, 4), devices)
    totals, far_below = lax.optimization_barrier((totals, far_below))
    means = totals * (coupling / (2.0 * GX * GY * GZ))
    far = window(1 - own_step, (0, ORB), far_below, far_pieces, far_above, targets, warm, ring)
    far_sides = sent(jnp.concatenate([far[:, :EDGE], far[:, EDGE + planes :]], axis=1))
    out = final_sum(means, own, more, far, own_sides + far_sides, own_pieces, far_pieces)
    out = out.transpose(0, 2, 1, 3).reshape(count, GZ, rows)
    return jnp.swapaxes(out, 1, 2)


def body(targets, partner_pool, owners, warm_start):
    rows = targets.shape[1]
    planes = rows // GY
    whole_planes = rows % GY == 0 and planes % 2 == 0 and planes > 2 * EDGE
    if whole_planes and GY == GZ and lax.axis_size("domain") % 4 == 0 and lax.axis_size("band") == 2:
        return plane_body(targets, partner_pool, owners, warm_start)
    return sweep_body(targets, partner_pool, owners, warm_start)


def solution(mesh):
    return jax.shard_map(
        body,
        mesh=mesh,
        in_specs=(
            P("band", "domain", None),
            P("band", "domain", None),
            P(),
            P(None, None, "band", "domain", None),
        ),
        out_specs=P("band", "domain", None),
        check_vma=False,
    )
```
